512 devices in a mesh: rep: 32 (over z, y_lo, core), tp: 16 (over x, y_hi).
Axes of the slice: x: 4, y: 8 (y_hi: 4, y_lo: 2; y = y_hi * 2 + y_lo), z: 8, core: 2. Of those that a mesh axis runs over, the one named last changes fastest.
Arguments:
- projected: bfloat16 [32, 256, 5120], P('rep', None, 'tp'), may hold values from -12 to 12
- serve_order: int32 [32, 256], P('rep'), may hold values from 0 to 255, each once within a row
- key_pool: bfloat16 [32, 512, 64, 512], P('rep', 'tp'), may hold values from -12 to 12
- value_pool: bfloat16 [32, 512, 64, 512], P('rep', 'tp'), may hold values from -4 to 4
- block_table: int32 [32, 256, 8], P('rep', 'tp'), may hold values from 0 to 31
- context_len: int32 [32, 256], P('rep', 'tp'), may hold values from 1 to 512, as said below
- partner: int32 [32], replicated, may hold values from 0 to 31, as said below
- moving_block: int32 [32, 16], P('rep', 'tp'), may hold values from 0 to 31, as said below
Outputs:
- attended: bfloat16 [32, 256, 4096], P('rep', None, 'tp')
The draws below stay inside these ranges and needn't reach their ends.
Inputs may be any that keep to these rules, and one draw needn't show every extreme that they name: `context_len`: some request of each replica has exactly 512 cached tokens. partner is a perfect matching of the replicas: partner[partner[r]] = r and partner[r] != r. moving_block[r, t] is the first block-table entry of slot t * 16 of replica r.
All inputs are finite; a program needn't handle non-finite values.
Results may differ from the reference program's by a relative error of at most 0.0049.
Values may be sent and summed in bfloat16 or wider, within the bound.
No kernel may reach another device: no remote copies, remote signals or barrier semaphores. Data moves between devices by JAX's collectives and lax.ppermute only.
A program may use at most 128 MiB of HBM per device.

```python
import jax
import jax.numpy as jnp
from jax import lax

H = 32
KVH = 4
HD = 128
QKV = 5120
BLOCK = 64
NBLK = 32
TBL = 8
ROWS = 16
TOKG = 256
N_REP = 32
N_TP = 16


def table_entries(key):
    return jax.random.randint(jax.random.fold_in(key, 11), (N_REP, TOKG, TBL), 0, NBLK).astype(jnp.int32)


def draw_projected(key, part):
    key = jax.random.fold_in(key, 3)
    first, second, third = jax.random.split(key, 3)
    queries = 2.0 * jax.random.truncated_normal(first, -4.0, 4.0, (N_REP, TOKG, KVH, H // KVH, HD), jnp.float32)
    fresh_keys = jax.random.truncated_normal(second, -4.0, 4.0, (N_REP, TOKG, KVH, HD), jnp.float32)
    fresh_values = jax.random.truncated_normal(third, -4.0, 4.0, (N_REP, TOKG, KVH, HD), jnp.float32)
    joined = jnp.concatenate([queries.reshape(N_REP, TOKG, H * HD), fresh_keys.reshape(N_REP, TOKG, KVH * HD), fresh_values.reshape(N_REP, TOKG, KVH * HD)], axis=-1)
    return joined.astype(jnp.bfloat16)


def draw_key_pool(key, part):
    key = jax.random.fold_in(key, 5)
    first = jax.random.fold_in(key, 0)
    shape = (N_REP, N_TP * NBLK, BLOCK, KVH, HD)
    keys = jax.random.truncated_normal(first, -4.0, 4.0, shape, jnp.float32)
    return keys.reshape(N_REP, N_TP * NBLK, BLOCK, KVH * HD).astype(jnp.bfloat16)


def draw_block_table(key, part):
    tables = table_entries(key)
    return tables


def draw_moving_block(key, part):
    tables = table_entries(key)
    return tables[:, ::ROWS, 0].astype(jnp.int32)


def draw_context_len(key, part):
    key = jax.random.fold_in(key, 7)
    first, second, third = jax.random.split(key, 3)
    most = TBL * BLOCK
    caps = jax.random.randint(first, (N_REP, N_TP, 1), most // 4, most + 1)
    lengths = jax.random.randint(second, (N_REP, N_TP, ROWS), 1, caps + 1).reshape(N_REP, TOKG)
    chosen = jax.random.randint(third, (N_REP, 1), 0, TOKG)
    slots = jnp.arange(TOKG, dtype=jnp.int32)[None, :]
    return jnp.where(slots == chosen, most, lengths).astype(jnp.int32)


def draw_partner(key, part):
    key = jax.random.fold_in(key, 9)
    first, second = jax.random.split(key, 2)
    half = N_REP // 2
    anchor = jax.random.randint(first, (), 0, N_REP).astype(jnp.int32)
    mate = ((anchor + half) % N_REP).astype(jnp.int32)
    steps = jnp.arange(N_REP - 2, dtype=jnp.int32)
    offsets = 1 + steps + jnp.where(steps + 1 >= half, 1, 0).astype(jnp.int32)
    others = (anchor + offsets) % N_REP
    others = jax.random.permutation(second, others)
    order = jnp.concatenate([anchor[None], mate[None], others]).astype(jnp.int32)
    evens = order[0::2]
    odds = order[1::2]
    matched = jnp.zeros((N_REP,), jnp.int32).at[evens].set(odds).at[odds].set(evens)
    return matched.astype(jnp.int32)


def block_levels(key, extent, pieces, smallest, largest):
    def one(position, blocks):
        steps = jax.random.uniform(jax.random.fold_in(jax.random.fold_in(key, 6), position), (blocks,), jnp.float32, smallest / len(pieces), largest / len(pieces))
        return jnp.repeat(jnp.exp(steps), extent[position] // blocks).reshape((-1,) + (1,) * (len(extent) - position - 1))

    loudness = one(*pieces[0])
    for cut in pieces[1:]:
        loudness = loudness * one(*cut)
    return loudness


def gaussian(rng, shape, scale, bound, cuts=(), kind=jnp.bfloat16):
    array = jax.random.normal(rng, shape, jnp.float32) * scale
    if len(cuts) > 0:
        array = block_levels(rng, shape, cuts, -0.22, 0.18) * array
    return jnp.clip(array, min=-bound, max=bound).astype(kind)


def setup_inputs(seed: int = 0) -> dict:
    arg_keys = jax.random.split(jax.random.key(seed), 9)
    return {
        "projected": draw_projected(jax.random.fold_in(arg_keys[8], 71), 0),
        "serve_order": jax.vmap(lambda own: jax.random.permutation(own, TOKG))(jax.random.split(arg_keys[1], N_REP)).reshape((N_REP, TOKG)).astype(jnp.int32),
        "key_pool": draw_key_pool(jax.random.fold_in(arg_keys[8], 71), 0),
        "value_pool": gaussian(arg_keys[3], (N_REP, N_TP * NBLK, BLOCK, KVH * HD), 1.0, 4.0, ((0, 32), (1, 16))),
        "block_table": draw_block_table(jax.random.fold_in(arg_keys[8], 71), 0),
        "context_len": draw_context_len(jax.random.fold_in(arg_keys[8], 71), 0),
        "partner": draw_partner(jax.random.fold_in(arg_keys[8], 71), 0),
        "moving_block": draw_moving_block(jax.random.fold_in(arg_keys[8], 71), 0),
    }


def attend(queries, fresh_keys, fresh_values, keys, values, valid):
    scale = 1.0 / jnp.sqrt(jnp.float32(queries.shape[-1]))
    queries = queries.astype(jnp.float32)
    scores = jnp.einsum('rkgd,rlkd->rkgl', queries, keys.astype(jnp.float32)) * scale
    fresh = jnp.einsum('rkgd,rkd->rkg', queries, fresh_keys.astype(jnp.float32)) * scale
    mask = valid[:, None, None, :]
    top = jnp.maximum(lax.optimization_barrier(jnp.max(jnp.where(mask, scores, -jnp.inf), axis=-1)), fresh)
    weights = jnp.where(mask, jnp.exp(scores - top[..., None]), 0.0).astype(jnp.bfloat16).astype(jnp.float32)
    own = jnp.exp(fresh - top).astype(jnp.bfloat16).astype(jnp.float32)
    total = lax.optimization_barrier(jnp.sum(weights, axis=-1)) + own
    numer = jnp.einsum('rkgl,rlkd->rkgd', weights, values.astype(jnp.float32))
    numer = numer + own[..., None] * fresh_values.astype(jnp.float32)[:, :, None, :]
    result = (numer / total[..., None]).astype(jnp.bfloat16)
    return result.reshape(result.shape[0], -1)

def serve_device(rows, key_blocks, value_blocks, tables, lengths):
    count = rows.shape[0]
    queries = rows[:, :H * HD].reshape(count, KVH, H // KVH, HD)
    fresh_keys = rows[:, H * HD:(H + KVH) * HD].reshape(count, KVH, HD)
    fresh_values = rows[:, (H + KVH) * HD:].reshape(count, KVH, HD)
    keys = key_blocks[tables].reshape(count, TBL * BLOCK, KVH, HD)
    values = value_blocks[tables].reshape(count, TBL * BLOCK, KVH, HD)
    positions = jnp.arange(TBL * BLOCK, dtype=jnp.int32)
    valid = positions[None, :] < lengths[:, None]
    return attend(queries, fresh_keys, fresh_values, keys, values, valid)

def reference(projected, serve_order, key_pool, value_pool, block_table, context_len, partner, moving_block):
    devices = jnp.arange(N_TP, dtype=jnp.int32)

    def one_replica(replica):
        mate = partner[replica]
        own_keys = key_pool[replica].reshape(N_TP, NBLK, BLOCK, KVH * HD)
        own_values = value_pool[replica].reshape(N_TP, NBLK, BLOCK, KVH * HD)
        mate_keys = key_pool[mate].reshape(N_TP, NBLK, BLOCK, KVH * HD)
        mate_values = value_pool[mate].reshape(N_TP, NBLK, BLOCK, KVH * HD)
        mine = moving_block[replica]
        theirs = moving_block[mate]
        own_keys = own_keys.at[devices, mine].set(mate_keys[devices, theirs])
        own_values = own_values.at[devices, mine].set(mate_values[devices, theirs])
        order_row = serve_order[replica]
        rows = projected[replica][order_row].reshape(N_TP, ROWS, QKV)
        tables = block_table[replica].reshape(N_TP, ROWS, TBL)
        lengths = context_len[replica].reshape(N_TP, ROWS)
        served = jax.vmap(serve_device)(rows, own_keys, own_values, tables, lengths)
        served = served.reshape(TOKG, H * HD)
        return jnp.zeros((TOKG, H * HD), served.dtype).at[order_row].set(served)
    return lax.map(one_replica, jnp.arange(N_REP, dtype=jnp.int32))
```

```python
import math

import jax
import jax.numpy as jnp
from jax import lax
from jax.experimental import pallas as pl
from jax.experimental.pallas import tpu as pltpu
from jax.sharding import PartitionSpec as P

H = 32
KVH = 4
GROUP = H // KVH
HD = 128
BLOCK = 64
NBLK = 32
TBL = 8
ROWS = 16
TOKG = 256
N_TP = 16
FEATS = 320
FRAME = 384
PIECES = 32
TOKENS = NBLK * BLOCK
NEG = -1e30
TO_EXP2 = math.log2(math.e) / math.sqrt(HD)
VMEM = pl.BlockSpec(memory_space=pltpu.VMEM)
SMEM = pl.BlockSpec(memory_space=pltpu.SMEM)
LIMIT = pltpu.CompilerParams(vmem_limit_bytes=40 * 1024 * 1024)


def piece(index):
    rows = (index % 16) // KVH * 16
    cols = index % KVH * HD
    return slice(rows, rows + 16), slice(cols, cols + HD)


def extract_kernel(block_id, keys, values, out):
    for index in range(PIECES):
        source = keys if index < PIECES // 2 else values
        rows, cols = piece(index)
        out[index] = source[0, 0, rows, cols]


def extract(key_pool, value_pool, moving_block):
    spec = pl.BlockSpec((1, 1, BLOCK, KVH * HD), lambda i, block_id: (0, block_id[0, 0], 0, 0))
    return pl.pallas_call(
        extract_kernel,
        out_shape=jax.ShapeDtypeStruct((PIECES, 16, HD), jnp.bfloat16),
        grid_spec=pltpu.PrefetchScalarGridSpec(
            num_scalar_prefetch=1,
            grid=(1,),
            in_specs=[spec, spec],
            out_specs=pl.BlockSpec((PIECES, 16, HD), lambda i, block_id: (0, 0, 0)),
        ),
        name="extract",
    )(moving_block, key_pool, value_pool)


def forward_kernel(partner, got, out):
    for replica in range(PIECES):
        out[replica] = got[partner[replica]]


def forward(partner, got):
    return pl.pallas_call(
        forward_kernel,
        out_shape=jax.ShapeDtypeStruct(got.shape, got.dtype),
        in_specs=[SMEM, VMEM],
        out_specs=VMEM,
        name="forward",
    )(partner, got)


def picks(order):
    request = lax.broadcasted_iota(jnp.int32, (TOKG, TOKG), 0)
    return jnp.where(request == order, 1.0, 0.0).astype(jnp.bfloat16)


def rows_kernel(order, features, out, frame):
    odd = lax.axis_index("tp") % 2
    frame[...] = jnp.zeros_like(frame)
    frame[pl.ds(pl.multiple_of(odd * 64, 64), FEATS), :] = features[0]
    rows = lax.dot_general(
        picks(order[...]), frame[...], (((0,), (1,)), ((), ())), preferred_element_type=jnp.float32
    )
    out[...] = rows.astype(jnp.bfloat16).reshape(out.shape)


def slot_rows(order, projected):
    return pl.pallas_call(
        rows_kernel,
        out_shape=jax.ShapeDtypeStruct((N_TP, ROWS, FRAME), jnp.bfloat16),
        in_specs=[VMEM, VMEM],
        out_specs=VMEM,
        scratch_shapes=[pltpu.VMEM((FRAME, TOKG), jnp.bfloat16)],
        cost_estimate=pl.CostEstimate(flops=2 * TOKG * TOKG * FRAME, bytes_accessed=400000, transcendentals=0),
        name="slot_rows",
    )(order, projected)


def lanes(served, tile):
    pair, place = divmod(tile, 5)
    even, odd = 2 * pair, 2 * pair + 1
    if place < 2:
        return served[even, :, place * HD : (place + 1) * HD]
    if place > 2:
        return served[odd, :, (place - 2) * HD : (place - 1) * HD]
    return served[even, :, 2 * HD : 3 * HD] + served[odd, :, 0:HD]


def counts(tables, lengths, block, offset):
    total = jnp.zeros((ROWS, block.shape[1]), jnp.float32)
    for entry in range(TBL):
        hit = (tables[:, entry : entry + 1] == block) & (offset < lengths - entry * BLOCK)
        total = total + jnp.where(hit, 1.0, 0.0)
    return total


def attend_kernel(block_id, served, keys, values, tables, lengths, numer, stats, queries):
    token = lax.broadcasted_iota(jnp.int32, (1, TOKENS), 1)
    block, offset = token // BLOCK, token % BLOCK
    block = jnp.where(block == block_id[0, 0], -1, block)
    count = counts(tables[0], lengths[...], block, offset)
    kept = count > 0.0
    ones = jnp.ones((TOKENS, HD), jnp.bfloat16)
    for head in range(KVH):
        rows = jnp.concatenate([lanes(served, head * GROUP + g) for g in range(GROUP)], axis=0)
        queries[head] = rows
        fresh_key = lanes(served, H + head).astype(jnp.float32)
        fresh_value = lanes(served, H + KVH + head).astype(jnp.float32)
        cols = slice(head * HD, (head + 1) * HD)
        key = keys[0, :, :, cols].reshape(TOKENS, HD)
        value = values[0, :, :, cols].reshape(TOKENS, HD)
        score = lax.dot_general(rows, key, (((1,), (1,)), ((), ())), preferred_element_type=jnp.float32)
        score = jnp.where(kept[None], score.reshape(GROUP, ROWS, TOKENS), NEG)
        fresh = jnp.sum(
            rows.astype(jnp.float32).reshape(GROUP, ROWS, HD) * fresh_key[None], axis=-1, keepdims=True
        )
        top = jnp.maximum(jnp.max(score, axis=-1, keepdims=True), fresh)
        weight = jnp.exp2((score - top) * TO_EXP2).astype(jnp.bfloat16)
        weight = (weight.astype(jnp.float32) * count[None]).astype(jnp.bfloat16).reshape(GROUP * ROWS, TOKENS)
        both = jnp.dot(weight, jnp.concatenate([value, ones], axis=1), preferred_element_type=jnp.float32)
        own = jnp.exp2((fresh - top) * TO_EXP2).astype(jnp.bfloat16).astype(jnp.float32)
        numer[head] = (both[:, :HD].reshape(GROUP, ROWS, HD) + own * fresh_value[None]).reshape(GROUP * ROWS, HD)
        total = both[:, HD:].reshape(GROUP, ROWS, HD) + own
        half = lax.broadcasted_iota(jnp.int32, (GROUP, ROWS, HD), 2) < HD // 2
        stats[head] = jnp.where(half, top, total).reshape(GROUP * ROWS, HD)


def attend(moving_block, served, key_pool, value_pool, tables, lengths):
    rows = GROUP * ROWS
    return pl.pallas_call(
        attend_kernel,
        out_shape=(
            jax.ShapeDtypeStruct((KVH, rows, HD), jnp.float32),
            jax.ShapeDtypeStruct((KVH, rows, HD), jnp.float32),
            jax.ShapeDtypeStruct((KVH, rows, HD), jnp.bfloat16),
        ),
        in_specs=[SMEM, VMEM, VMEM, VMEM, VMEM, VMEM],
        out_specs=(VMEM, VMEM, VMEM),
        compiler_params=LIMIT,
        cost_estimate=pl.CostEstimate(
            flops=4 * KVH * rows * TOKENS * HD, bytes_accessed=5000000, transcendentals=KVH * rows * TOKENS
        ),
        name="attend",
    )(moving_block, served, key_pool, value_pool, tables, lengths)


def merge_kernel(block_id, arrived, numer, stats, queries, tables, lengths, out):
    offset = lax.broadcasted_iota(jnp.int32, (1, BLOCK), 1)
    count = counts(tables[0], lengths[...], jnp.full((1, BLOCK), block_id[0, 0], jnp.int32), offset)
    kept = count > 0.0
    ones = jnp.ones((BLOCK, HD), jnp.bfloat16)
    for head in range(KVH):
        key = jnp.concatenate([arrived[4 * a + head] for a in range(4)], axis=0)
        value = jnp.concatenate([arrived[16 + 4 * a + head] for a in range(4)], axis=0)
        score = lax.dot_general(
            queries[head], key, (((1,), (1,)), ((), ())), preferred_element_type=jnp.float32
        )
        score = jnp.where(kept[None], score.reshape(GROUP, ROWS, BLOCK), NEG)
        stat = stats[head].reshape(GROUP, ROWS, HD)
        before, total = stat[:, :, 0:1], stat[:, :, HD - 1 : HD]
        top = jnp.maximum(jnp.max(score, axis=-1, keepdims=True), before)
        weight = jnp.exp2((score - top) * TO_EXP2).astype(jnp.bfloat16)
        weight = (weight.astype(jnp.float32) * count[None]).astype(jnp.bfloat16).reshape(GROUP * ROWS, BLOCK)
        both = jnp.dot(weight, jnp.concatenate([value, ones], axis=1), preferred_element_type=jnp.float32)
        both = both.reshape(GROUP, ROWS, 2 * HD)
        kept_part = jnp.exp2((before - top) * TO_EXP2)
        result = (numer[head].reshape(GROUP, ROWS, HD) * kept_part + both[:, :, :HD]) / (
            total * kept_part + both[:, :, HD:]
        )
        result = result.astype(jnp.bfloat16)
        for g in range(GROUP):
            out[4 * head + g // 2, :, (g % 2) * HD : (g % 2 + 1) * HD] = result[g]


def merge(moving_block, arrived, numer, stats, queries, tables, lengths):
    return pl.pallas_call(
        merge_kernel,
        out_shape=jax.ShapeDtypeStruct((N_TP, ROWS, 2 * HD), jnp.bfloat16),
        in_specs=[SMEM, VMEM, VMEM, VMEM, VMEM, VMEM, VMEM],
        out_specs=VMEM,
        compiler_params=LIMIT,
        name="merge",
    )(moving_block, arrived, numer, stats, queries, tables, lengths)


def place_kernel(order, returned, out):
    rows = returned[...].reshape(TOKG, 2 * HD)
    out[0] = jnp.dot(picks(order[...]), rows, preferred_element_type=jnp.float32).astype(jnp.bfloat16)


def place(order, returned):
    return pl.pallas_call(
        place_kernel,
        out_shape=jax.ShapeDtypeStruct((1, TOKG, 2 * HD), jnp.bfloat16),
        in_specs=[VMEM, VMEM],
        out_specs=VMEM,
        name="place",
    )(order, returned)


def exchange(slots, axis):
    return lax.all_to_all(slots, axis, split_axis=0, concat_axis=0, tiled=True)


def body(
    projected, serve_order, key_pool, value_pool, block_table, context_len, partner, moving_block
):
    lengths = context_len.reshape(ROWS, 1)
    spread = exchange(extract(key_pool, value_pool, moving_block), "rep")
    served = exchange(slot_rows(serve_order, jnp.swapaxes(projected, 1, 2)), "tp")
    arrived = exchange(forward(partner, spread), "rep")
    numer, stats, queries = attend(moving_block, served, key_pool, value_pool, block_table, lengths)
    heads = merge(moving_block, arrived, numer, stats, queries, block_table, lengths)
    return place(serve_order, exchange(heads, "tp"))


def solution(mesh):
    in_specs = (
        P("rep", None, "tp"),
        P("rep", None),
        P("rep", "tp", None, None),
        P("rep", "tp", None, None),
        P("rep", "tp", None),
        P("rep", "tp"),
        P(),
        P("rep", "tp"),
    )
    out_specs = P("rep", None, "tp")
    return jax.shard_map(body, mesh=mesh, in_specs=in_specs, out_specs=out_specs, check_vma=False)
```

```python
import math

import jax
import jax.numpy as jnp
from jax import lax
from jax.experimental import pallas as pl
from jax.experimental.pallas import tpu as pltpu
from jax.sharding import PartitionSpec as P

H = 32
KVH = 4
GROUP = H // KVH
HD = 128
BLOCK = 64
NBLK = 32
TBL = 8
ROWS = 16
TOKG = 256
N_TP = 16
FEATS = 320
FRAME = 384
PIECES = 32
SPANS = BLOCK // 16
TOKENS = NBLK * BLOCK
NEG = -1e30
TO_EXP2 = math.log2(math.e) / math.sqrt(HD)
VMEM = pl.BlockSpec(memory_space=pltpu.VMEM)
HBM = pl.BlockSpec(memory_space=pltpu.HBM)
SMEM = pl.BlockSpec(memory_space=pltpu.SMEM)
SMALL = pltpu.CompilerParams(vmem_limit_bytes=8 * 1024 * 1024)
LARGE = pltpu.CompilerParams(vmem_limit_bytes=24 * 1024 * 1024)


def in_vmem(array):
    return pltpu.with_memory_space_constraint(array, pltpu.VMEM)


def in_hbm(array):
    return pltpu.with_memory_space_constraint(array, pltpu.HBM)


def extract_kernel(block_id, keys, values, out, near, sems):
    copies = []
    for index in range(2 * SPANS):
        pool, span = (keys, values)[index // SPANS], index % SPANS
        copies.append(pltpu.make_async_copy(pool.at[block_id[0, 0], span], near.at[index], sems.at[index]))
        copies[-1].start()
    for index, copy in enumerate(copies):
        copy.wait()
        for head in range(KVH):
            out[KVH * index + head] = near[index, :, head * HD : (head + 1) * HD]


def extract(key_pool, value_pool, moving_block):
    pool = (NBLK, SPANS, 16, KVH * HD)
    return pl.pallas_call(
        extract_kernel,
        out_shape=pltpu.VMEM((PIECES, 16, HD), jnp.bfloat16),
        in_specs=[SMEM, HBM, HBM],
        out_specs=VMEM,
        scratch_shapes=[
            pltpu.VMEM((2 * SPANS, 16, KVH * HD), jnp.bfloat16),
            pltpu.SemaphoreType.DMA((2 * SPANS,)),
        ],
        compiler_params=SMALL,
        name="extract",
    )(moving_block, in_hbm(key_pool.reshape(pool)), in_hbm(value_pool.reshape(pool)))


def forward_kernel(partner, got, out):
    for replica in range(PIECES):
        out[replica] = got[partner[replica]]


def forward(partner, got):
    return pl.pallas_call(
        forward_kernel,
        out_shape=pltpu.VMEM(got.shape, got.dtype),
        in_specs=[SMEM, VMEM],
        out_specs=VMEM,
        compiler_params=SMALL,
        name="forward",
    )(partner, in_vmem(got))


def picks(order):
    request = lax.broadcasted_iota(jnp.int32, (TOKG, TOKG), 0)
    return jnp.where(request == order, 1.0, 0.0).astype(jnp.bfloat16)


def rows_kernel(order, features, out, chosen, frame):
    odd = lax.axis_index("tp") % 2
    frame[...] = jnp.zeros_like(frame)
    frame[pl.ds(pl.multiple_of(odd * 64, 64), FEATS), :] = features[0]
    chosen[...] = picks(order[...])
    rows = lax.dot_general(
        chosen[...], frame[...], (((0,), (1,)), ((), ())), preferred_element_type=jnp.float32
    )
    out[...] = rows.astype(jnp.bfloat16).reshape(out.shape)


def slot_rows(order, projected):
    return pl.pallas_call(
        rows_kernel,
        out_shape=(pltpu.VMEM((N_TP, ROWS, FRAME), jnp.bfloat16), pltpu.VMEM((TOKG, TOKG), jnp.bfloat16)),
        in_specs=[VMEM, VMEM],
        out_specs=(VMEM, VMEM),
        scratch_shapes=[pltpu.VMEM((FRAME, TOKG), jnp.bfloat16)],
        cost_estimate=pl.CostEstimate(flops=2 * TOKG * TOKG * FRAME, bytes_accessed=400000, transcendentals=0),
        compiler_params=SMALL,
        name="slot_rows",
    )(order, projected)


def lanes(served, tile):
    pair, place = divmod(tile, 5)
    even, odd = 2 * pair, 2 * pair + 1
    if place < 2:
        return served[even, :, place * HD : (place + 1) * HD]
    if place > 2:
        return served[odd, :, (place - 2) * HD : (place - 1) * HD]
    return served[even, :, 2 * HD : 3 * HD] + served[odd, :, 0:HD]


def counts(tables, lengths, block, offset):
    total = jnp.zeros((ROWS, block.shape[1]), jnp.float32)
    for entry in range(TBL):
        hit = (tables[:, entry : entry + 1] == block) & (offset < lengths - entry * BLOCK)
        total = total + jnp.where(hit, 1.0, 0.0)
    return total


def attend_kernel(
    block_id, served, keys, value_pool, tables, lengths, numer, tops, totals, queries, moved, values, sem
):
    fetch = pltpu.make_async_copy(value_pool, values, sem)
    fetch.start()
    moved[...] = counts(
        jnp.where(tables[0] == block_id[...], 0, -1), lengths[...], jnp.zeros((1, BLOCK), jnp.int32),
        lax.broadcasted_iota(jnp.int32, (1, BLOCK), 1),
    )
    token = lax.broadcasted_iota(jnp.int32, (1, TOKENS), 1)
    block, offset = token // BLOCK, token % BLOCK
    block = jnp.where(block == block_id[...], -1, block)
    count = counts(tables[0], lengths[...], block, offset)
    kept = count > 0.0
    ones = jnp.ones((TOKENS, HD), jnp.bfloat16)
    for head in range(KVH):
        rows = jnp.concatenate([lanes(served, head * GROUP + g) for g in range(GROUP)], axis=0)
        queries[head] = rows
        fresh_key = lanes(served, H + head).astype(jnp.float32)
        fresh_value = lanes(served, H + KVH + head).astype(jnp.float32)
        cols = slice(head * HD, (head + 1) * HD)
        key = keys[0, :, :, cols].reshape(TOKENS, HD)
        score = lax.dot_general(rows, key, (((1,), (1,)), ((), ())), preferred_element_type=jnp.float32)
        score = jnp.where(kept[None], score.reshape(GROUP, ROWS, TOKENS), NEG)
        fresh = jnp.sum(
            rows.astype(jnp.float32).reshape(GROUP, ROWS, HD) * fresh_key[None], axis=-1, keepdims=True
        )
        top = jnp.maximum(jnp.max(score, axis=-1, keepdims=True), fresh)
        weight = jnp.exp2((score - top) * TO_EXP2).astype(jnp.bfloat16)
        weight = (weight.astype(jnp.float32) * count[None]).astype(jnp.bfloat16).reshape(GROUP * ROWS, TOKENS)
        if head == 0:
            fetch.wait()
        value = values[0, :, :, cols].reshape(TOKENS, HD)
        both = jnp.dot(weight, jnp.concatenate([value, ones], axis=1), preferred_element_type=jnp.float32)
        own = jnp.exp2((fresh - top) * TO_EXP2).astype(jnp.bfloat16).astype(jnp.float32)
        numer[head] = (both[:, :HD].reshape(GROUP, ROWS, HD) + own * fresh_value[None]).reshape(GROUP * ROWS, HD)
        total = both[:, HD:].reshape(GROUP, ROWS, HD) + own
        tops[head] = jnp.broadcast_to(top, (GROUP, ROWS, HD)).reshape(GROUP * ROWS, HD)
        totals[head] = total.reshape(GROUP * ROWS, HD)


def attend(moving_block, served, key_pool, value_pool, tables, lengths):
    rows = GROUP * ROWS
    return pl.pallas_call(
        attend_kernel,
        out_shape=(
            pltpu.VMEM((KVH, rows, HD), jnp.float32),
            pltpu.VMEM((KVH, rows, HD), jnp.float32),
            pltpu.VMEM((KVH, rows, HD), jnp.float32),
            pltpu.VMEM((KVH, rows, HD), jnp.bfloat16),
            pltpu.VMEM((ROWS, BLOCK), jnp.float32),
        ),
        in_specs=[VMEM, VMEM, VMEM, HBM, VMEM, VMEM],
        out_specs=(VMEM,) * 5,
        scratch_shapes=[
            pltpu.VMEM((1, NBLK, BLOCK, KVH * HD), jnp.bfloat16),
            pltpu.SemaphoreType.DMA,
        ],
        compiler_params=LARGE,
        cost_estimate=pl.CostEstimate(
            flops=4 * KVH * rows * TOKENS * HD, bytes_accessed=5000000, transcendentals=KVH * rows * TOKENS
        ),
        name="attend",
    )(moving_block, in_vmem(served), in_vmem(key_pool), in_hbm(value_pool), tables, lengths)


def merge_kernel(arrived, numer, tops, totals, queries, moved, out):
    count = moved[...]
    kept = count > 0.0
    ones = jnp.ones((BLOCK, HD), jnp.bfloat16)
    scores = []
    for head in range(KVH):
        key = jnp.concatenate([arrived[KVH * span + head] for span in range(SPANS)], axis=0)
        score = lax.dot_general(
            queries[head], key, (((1,), (1,)), ((), ())), preferred_element_type=jnp.float32
        )
        scores.append(jnp.where(kept[None], score.reshape(GROUP, ROWS, BLOCK), NEG))
    befores = [tops[head].reshape(GROUP, ROWS, HD) for head in range(KVH)]
    highest = [jnp.max(score, axis=-1, keepdims=True) for score in scores]
    latest = [jnp.maximum(new, old) for new, old in zip(highest, befores)]
    both = []
    for head in range(KVH):
        weight = jnp.exp2((scores[head] - latest[head][:, :, :BLOCK]) * TO_EXP2).astype(jnp.bfloat16)
        weight = (weight.astype(jnp.float32) * count[None]).astype(jnp.bfloat16).reshape(GROUP * ROWS, BLOCK)
        value = jnp.concatenate([arrived[KVH * (SPANS + span) + head] for span in range(SPANS)], axis=0)
        part = jnp.dot(weight, jnp.concatenate([value, ones], axis=1), preferred_element_type=jnp.float32)
        both.append(part.reshape(GROUP, ROWS, 2 * HD))
    results = []
    for head in range(KVH):
        kept_part = jnp.exp2((befores[head] - latest[head]) * TO_EXP2)
        top = numer[head].reshape(GROUP, ROWS, HD) * kept_part + both[head][:, :, :HD]
        bottom = totals[head].reshape(GROUP, ROWS, HD) * kept_part + both[head][:, :, HD:]
        results.append((top / bottom).astype(jnp.bfloat16))
    for head in range(KVH):
        for g in range(GROUP):
            out[4 * head + g // 2, :, (g % 2) * HD : (g % 2 + 1) * HD] = results[head][g]


def merge(arrived, numer, tops, totals, queries, moved):
    return pl.pallas_call(
        merge_kernel,
        out_shape=pltpu.VMEM((N_TP, ROWS, 2 * HD), jnp.bfloat16),
        in_specs=[VMEM] * 6,
        out_specs=VMEM,
        compiler_params=SMALL,
        name="merge",
    )(in_vmem(arrived), numer, tops, totals, queries, moved)


def place_kernel(chosen, returned, out, rows, sems):
    slots = returned[...].reshape(TOKG, 2 * HD)
    half = TOKG // 2
    copies = []
    for part in range(2):
        here = slice(part * half, (part + 1) * half)
        rows[here] = jnp.dot(chosen[here], slots, preferred_element_type=jnp.float32).astype(jnp.bfloat16)
        copies.append(pltpu.make_async_copy(rows.at[here], out.at[0, here], sems.at[part]))
        copies[-1].start()
    for copy in copies:
        copy.wait()


def place(chosen, returned):
    return pl.pallas_call(
        place_kernel,
        out_shape=jax.ShapeDtypeStruct((1, TOKG, 2 * HD), jnp.bfloat16),
        in_specs=[VMEM, VMEM],
        out_specs=HBM,
        scratch_shapes=[pltpu.VMEM((TOKG, 2 * HD), jnp.bfloat16), pltpu.SemaphoreType.DMA((2,))],
        compiler_params=SMALL,
        name="place",
    )(chosen, in_vmem(returned))


def exchange(slots, axis):
    return lax.all_to_all(slots, axis, split_axis=0, concat_axis=0, tiled=True)


def body(
    projected, serve_order, key_pool, value_pool, block_table, context_len, partner, moving_block
):
    lengths = context_len.reshape(ROWS, 1)
    spread = exchange(extract(key_pool, value_pool, moving_block), "rep")
    rows, chosen = slot_rows(serve_order, jnp.swapaxes(projected, 1, 2))
    served = exchange(rows, "tp")
    arrived = exchange(forward(partner, spread), "rep")
    parts = attend(moving_block, served, key_pool, value_pool, block_table, lengths)
    return place(chosen, exchange(merge(arrived, *parts), "tp"))


def solution(mesh):
    in_specs = (
        P("rep", None, "tp"),
        P("rep", None),
        P("rep", "tp", None, None),
        P("rep", "tp", None, None),
        P("rep", "tp", None),
        P("rep", "tp"),
        P(),
        P("rep", "tp"),
    )
    out_specs = P("rep", None, "tp")
    return jax.shard_map(body, mesh=mesh, in_specs=in_specs, out_specs=out_specs, check_vma=False)
```

```python
import math

import jax
import jax.numpy as jnp
from jax import lax
from jax.experimental import pallas as pl
from jax.experimental.pallas import tpu as pltpu
from jax.sharding import PartitionSpec as P

H = 32
KVH = 4
GROUP = H // KVH
HD = 128
BLOCK = 64
NBLK = 32
TBL = 8
ROWS = 16
TOKG = 256
N_TP = 16
FEATS = 320
FRAME = 384
PIECES = 32
SPANS = BLOCK // 16
TOKENS = NBLK * BLOCK
NEG = -1e30
TO_EXP2 = math.log2(math.e) / math.sqrt(HD)
VMEM = pl.BlockSpec(memory_space=pltpu.VMEM)
HBM = pl.BlockSpec(memory_space=pltpu.HBM)
SMEM = pl.BlockSpec(memory_space=pltpu.SMEM)
SMALL = pltpu.CompilerParams(vmem_limit_bytes=8 * 1024 * 1024)
LARGE = pltpu.CompilerParams(vmem_limit_bytes=24 * 1024 * 1024)


def in_vmem(array):
    return pltpu.with_memory_space_constraint(array, pltpu.VMEM)


def in_hbm(array):
    return pltpu.with_memory_space_constraint(array, pltpu.HBM)


def extract_kernel(block_id, keys, values, out, near, sems):
    copies = []
    for index in range(2 * SPANS):
        pool, span = (keys, values)[index // SPANS], index % SPANS
        copies.append(pltpu.make_async_copy(pool.at[block_id[0, 0], span], near.at[index], sems.at[index]))
        copies[-1].start()
    for index, copy in enumerate(copies):
        copy.wait()
        for head in range(KVH):
            out[KVH * index + head] = near[index, :, head * HD : (head + 1) * HD]


def extract(key_pool, value_pool, moving_block):
    pool = (NBLK, SPANS, 16, KVH * HD)
    return pl.pallas_call(
        extract_kernel,
        out_shape=pltpu.VMEM((PIECES, 16, HD), jnp.bfloat16),
        in_specs=[SMEM, HBM, HBM],
        out_specs=VMEM,
        scratch_shapes=[
            pltpu.VMEM((2 * SPANS, 16, KVH * HD), jnp.bfloat16),
            pltpu.SemaphoreType.DMA((2 * SPANS,)),
        ],
        compiler_params=SMALL,
        name="extract",
    )(moving_block, in_hbm(key_pool.reshape(pool)), in_hbm(value_pool.reshape(pool)))


def forward_kernel(partner, got, after, out):
    for replica in range(PIECES):
        out[replica] = got[partner[replica]]


def forward(partner, got, after):
    return pl.pallas_call(
        forward_kernel,
        out_shape=pltpu.VMEM(got.shape, got.dtype),
        in_specs=[SMEM, VMEM, VMEM],
        out_specs=VMEM,
        compiler_params=SMALL,
        name="forward",
    )(partner, in_vmem(got), after)


def picks(order):
    request = lax.broadcasted_iota(jnp.int32, (TOKG, TOKG), 0)
    return jnp.where(request == order, 1.0, 0.0).astype(jnp.bfloat16)


def rows_kernel(order, features, out, chosen, frame, near, rows, sems):
    odd = lax.axis_index("tp") % 2
    fetch = [
        pltpu.make_async_copy(order, near, sems.at[0]),
        pltpu.make_async_copy(
            features.at[0], frame.at[pl.ds(pl.multiple_of(odd * 64, 64), FEATS), :], sems.at[1]
        ),
    ]
    for copy in fetch:
        copy.start()
    blank = jnp.zeros((FRAME - FEATS, TOKG), jnp.bfloat16)
    frame[pl.ds(pl.multiple_of((1 - odd) * FEATS, 64), FRAME - FEATS), :] = blank
    fetch[0].wait()
    chosen[...] = picks(near[...])
    fetch[1].wait()
    send = []
    for part in range(4):
        width = TOKG // 4
        picked = lax.dot_general(
            chosen[:, part * width : (part + 1) * width],
            frame[...],
            (((0,), (1,)), ((), ())),
            preferred_element_type=jnp.float32,
        )
        here = pl.ds(part * N_TP // 4, N_TP // 4)
        rows[here] = picked.astype(jnp.bfloat16).reshape(N_TP // 4, ROWS, FRAME)
        send.append(pltpu.make_async_copy(rows.at[here], out.at[here], sems.at[2 + part]))
        send[-1].start()
    for copy in send:
        copy.wait()


def slot_rows(order, projected):
    return pl.pallas_call(
        rows_kernel,
        out_shape=(
            jax.ShapeDtypeStruct((N_TP, ROWS, FRAME), jnp.bfloat16),
            pltpu.VMEM((TOKG, TOKG), jnp.bfloat16),
        ),
        in_specs=[HBM, HBM],
        out_specs=(HBM, VMEM),
        scratch_shapes=[
            pltpu.VMEM((FRAME, TOKG), jnp.bfloat16),
            pltpu.VMEM((1, TOKG), jnp.int32),
            pltpu.VMEM((N_TP, ROWS, FRAME), jnp.bfloat16),
            pltpu.SemaphoreType.DMA((6,)),
        ],
        cost_estimate=pl.CostEstimate(flops=2 * TOKG * TOKG * FRAME, bytes_accessed=400000, transcendentals=0),
        compiler_params=SMALL,
        name="slot_rows",
    )(in_hbm(order), in_hbm(projected))


def lanes(served, tile):
    pair, place = divmod(tile, 5)
    even, odd = 2 * pair, 2 * pair + 1
    if place < 2:
        return served[even, :, place * HD : (place + 1) * HD]
    if place > 2:
        return served[odd, :, (place - 2) * HD : (place - 1) * HD]
    return served[even, :, 2 * HD : 3 * HD] + served[odd, :, 0:HD]


def counts(tables, lengths, block, offset):
    total = jnp.zeros((ROWS, block.shape[1]), jnp.float32)
    for entry in range(TBL):
        hit = (tables[:, entry : entry + 1] == block) & (offset < lengths - entry * BLOCK)
        total = total + jnp.where(hit, 1.0, 0.0)
    return total


def attend_kernel(
    block_id, served, keys, value_pool, tables, lengths, numer, tops, totals, queries, moved, values, sem
):
    fetch = pltpu.make_async_copy(value_pool, values, sem)
    fetch.start()
    moved[...] = counts(
        jnp.where(tables[0] == block_id[...], 0, -1), lengths[...], jnp.zeros((1, BLOCK), jnp.int32),
        lax.broadcasted_iota(jnp.int32, (1, BLOCK), 1),
    )
    token = lax.broadcasted_iota(jnp.int32, (1, TOKENS), 1)
    block, offset = token // BLOCK, token % BLOCK
    block = jnp.where(block == block_id[...], -1, block)
    count = counts(tables[0], lengths[...], block, offset)
    kept = count > 0.0
    ones = jnp.ones((TOKENS, HD), jnp.bfloat16)
    for head in range(KVH):
        rows = jnp.concatenate([lanes(served, head * GROUP + g) for g in range(GROUP)], axis=0)
        queries[head] = rows
        fresh_key = lanes(served, H + head).astype(jnp.float32)
        fresh_value = lanes(served, H + KVH + head).astype(jnp.float32)
        cols = slice(head * HD, (head + 1) * HD)
        key = keys[0, :, :, cols].reshape(TOKENS, HD)
        score = lax.dot_general(rows, key, (((1,), (1,)), ((), ())), preferred_element_type=jnp.float32)
        score = jnp.where(kept[None], score.reshape(GROUP, ROWS, TOKENS), NEG)
        fresh = jnp.sum(
            rows.astype(jnp.float32).reshape(GROUP, ROWS, HD) * fresh_key[None], axis=-1, keepdims=True
        )
        top = jnp.maximum(jnp.max(score, axis=-1, keepdims=True), fresh)
        weight = jnp.exp2((score - top) * TO_EXP2).astype(jnp.bfloat16)
        weight = (weight.astype(jnp.float32) * count[None]).astype(jnp.bfloat16).reshape(GROUP * ROWS, TOKENS)
        if head == 0:
            fetch.wait()
        value = values[0, :, :, cols].reshape(TOKENS, HD)
        both = jnp.dot(weight, jnp.concatenate([value, ones], axis=1), preferred_element_type=jnp.float32)
        own = jnp.exp2((fresh - top) * TO_EXP2).astype(jnp.bfloat16).astype(jnp.float32)
        numer[head] = (both[:, :HD].reshape(GROUP, ROWS, HD) + own * fresh_value[None]).reshape(GROUP * ROWS, HD)
        total = both[:, HD:].reshape(GROUP, ROWS, HD) + own
        tops[head] = jnp.broadcast_to(top, (GROUP, ROWS, HD)).reshape(GROUP * ROWS, HD)
        totals[head] = total.reshape(GROUP * ROWS, HD)


def attend(moving_block, served, key_pool, value_pool, tables, lengths):
    rows = GROUP * ROWS
    return pl.pallas_call(
        attend_kernel,
        out_shape=(
            pltpu.VMEM((KVH, rows, HD), jnp.float32),
            pltpu.VMEM((KVH, rows, HD), jnp.float32),
            pltpu.VMEM((KVH, rows, HD), jnp.float32),
            pltpu.VMEM((KVH, rows, HD), jnp.bfloat16),
            pltpu.VMEM((ROWS, BLOCK), jnp.float32),
        ),
        in_specs=[VMEM, VMEM, VMEM, HBM, VMEM, VMEM],
        out_specs=(VMEM,) * 5,
        scratch_shapes=[
            pltpu.VMEM((1, NBLK, BLOCK, KVH * HD), jnp.bfloat16),
            pltpu.SemaphoreType.DMA,
        ],
        compiler_params=LARGE,
        cost_estimate=pl.CostEstimate(
            flops=4 * KVH * rows * TOKENS * HD, bytes_accessed=5000000, transcendentals=KVH * rows * TOKENS
        ),
        name="attend",
    )(moving_block, in_vmem(served), in_vmem(key_pool), in_hbm(value_pool), tables, lengths)


def merge_kernel(arrived, numer, tops, totals, queries, moved, out):
    count = moved[...]
    kept = count > 0.0
    ones = jnp.ones((BLOCK, HD), jnp.bfloat16)
    scores = []
    for head in range(KVH):
        key = jnp.concatenate([arrived[KVH * span + head] for span in range(SPANS)], axis=0)
        score = lax.dot_general(
            queries[head], key, (((1,), (1,)), ((), ())), preferred_element_type=jnp.float32
        )
        scores.append(jnp.where(kept[None], score.reshape(GROUP, ROWS, BLOCK), NEG))
    befores = [tops[head].reshape(GROUP, ROWS, HD) for head in range(KVH)]
    highest = [jnp.max(score, axis=-1, keepdims=True) for score in scores]
    latest = [jnp.maximum(new, old) for new, old in zip(highest, befores)]
    both = []
    for head in range(KVH):
        weight = jnp.exp2((scores[head] - latest[head][:, :, :BLOCK]) * TO_EXP2).astype(jnp.bfloat16)
        weight = (weight.astype(jnp.float32) * count[None]).astype(jnp.bfloat16).reshape(GROUP * ROWS, BLOCK)
        value = jnp.concatenate([arrived[KVH * (SPANS + span) + head] for span in range(SPANS)], axis=0)
        part = jnp.dot(weight, jnp.concatenate([value, ones], axis=1), preferred_element_type=jnp.float32)
        both.append(part.reshape(GROUP, ROWS, 2 * HD))
    results = []
    for head in range(KVH):
        kept_part = jnp.exp2((befores[head] - latest[head]) * TO_EXP2)
        top = numer[head].reshape(GROUP, ROWS, HD) * kept_part + both[head][:, :, :HD]
        bottom = totals[head].reshape(GROUP, ROWS, HD) * kept_part + both[head][:, :, HD:]
        results.append((top / bottom).astype(jnp.bfloat16))
    for head in range(KVH):
        for g in range(GROUP):
            out[4 * head + g // 2, :, (g % 2) * HD : (g % 2 + 1) * HD] = results[head][g]


def merge(arrived, numer, tops, totals, queries, moved):
    return pl.pallas_call(
        merge_kernel,
        out_shape=pltpu.VMEM((N_TP, ROWS, 2 * HD), jnp.bfloat16),
        in_specs=[VMEM] * 6,
        out_specs=VMEM,
        compiler_params=SMALL,
        name="merge",
    )(in_vmem(arrived), numer, tops, totals, queries, moved)


def place_kernel(chosen, returned, out, rows, sems):
    slots = returned[...].reshape(TOKG, 2 * HD)
    half = TOKG // 2
    copies = []
    for part in range(2):
        here = slice(part * half, (part + 1) * half)
        rows[here] = jnp.dot(chosen[here], slots, preferred_element_type=jnp.float32).astype(jnp.bfloat16)
        copies.append(pltpu.make_async_copy(rows.at[here], out.at[0, here], sems.at[part]))
        copies[-1].start()
    for copy in copies:
        copy.wait()


def place(chosen, returned):
    return pl.pallas_call(
        place_kernel,
        out_shape=jax.ShapeDtypeStruct((1, TOKG, 2 * HD), jnp.bfloat16),
        in_specs=[VMEM, VMEM],
        out_specs=HBM,
        scratch_shapes=[pltpu.VMEM((TOKG, 2 * HD), jnp.bfloat16), pltpu.SemaphoreType.DMA((2,))],
        compiler_params=SMALL,
        name="place",
    )(chosen, in_vmem(returned))


def exchange(slots, axis):
    return lax.all_to_all(slots, axis, split_axis=0, concat_axis=0, tiled=True)


def body(
    projected, serve_order, key_pool, value_pool, block_table, context_len, partner, moving_block
):
    lengths = context_len.reshape(ROWS, 1)
    rows, chosen = slot_rows(serve_order, jnp.swapaxes(projected, 1, 2))
    served = exchange(rows, "tp")
    spread = exchange(extract(key_pool, value_pool, moving_block), "rep")
    *parts, moved = attend(moving_block, served, key_pool, value_pool, block_table, lengths)
    arrived = exchange(forward(partner, spread, moved), "rep")
    return place(chosen, exchange(merge(arrived, *parts, moved), "tp"))


def solution(mesh):
    in_specs = (
        P("rep", None, "tp"),
        P("rep", None),
        P("rep", "tp", None, None),
        P("rep", "tp", None, None),
        P("rep", "tp", None),
        P("rep", "tp"),
        P(),
        P("rep", "tp"),
    )
    out_specs = P("rep", None, "tp")
    return jax.shard_map(body, mesh=mesh, in_specs=in_specs, out_specs=out_specs, check_vma=False)
```

```python
import math

import jax
import jax.numpy as jnp
from jax import lax
from jax.experimental import pallas as pl
from jax.experimental.pallas import tpu as pltpu
from jax.sharding import PartitionSpec as P

H = 32
KVH = 4
GROUP = H // KVH
HD = 128
BLOCK = 64
NBLK = 32
TBL = 8
ROWS = 16
TOKG = 256
N_TP = 16
FEATS = 320
FRAME = 384
PIECES = 32
SPANS = BLOCK // 16
TOKENS = NBLK * BLOCK
NEG = -1e30
TO_EXP2 = math.log2(math.e) / math.sqrt(HD)
VMEM = pl.BlockSpec(memory_space=pltpu.VMEM)
HBM = pl.BlockSpec(memory_space=pltpu.HBM)
SMEM = pl.BlockSpec(memory_space=pltpu.SMEM)
SMALL = pltpu.CompilerParams(vmem_limit_bytes=8 * 1024 * 1024)
LARGE = pltpu.CompilerParams(vmem_limit_bytes=24 * 1024 * 1024)


def in_vmem(array):
    return pltpu.with_memory_space_constraint(array, pltpu.VMEM)


def in_hbm(array):
    return pltpu.with_memory_space_constraint(array, pltpu.HBM)


def extract_kernel(block_id, partner, keys, values, out, mates, near, sems):
    for replica in range(PIECES):
        mates[replica] = partner[replica]
    copies = []
    for index in range(2 * SPANS):
        pool, span = (keys, values)[index // SPANS], index % SPANS
        copies.append(pltpu.make_async_copy(pool.at[block_id[0, 0], span], near.at[index], sems.at[index]))
        copies[-1].start()
    for index, copy in enumerate(copies):
        copy.wait()
        for head in range(KVH):
            out[KVH * index + head] = near[index, :, head * HD : (head + 1) * HD]


def extract(key_pool, value_pool, moving_block, partner):
    pool = (NBLK, SPANS, 16, KVH * HD)
    return pl.pallas_call(
        extract_kernel,
        out_shape=(pltpu.VMEM((PIECES, 16, HD), jnp.bfloat16), pltpu.SMEM((PIECES,), jnp.int32)),
        in_specs=[SMEM, SMEM, HBM, HBM],
        out_specs=(VMEM, SMEM),
        scratch_shapes=[
            pltpu.VMEM((2 * SPANS, 16, KVH * HD), jnp.bfloat16),
            pltpu.SemaphoreType.DMA((2 * SPANS,)),
        ],
        compiler_params=SMALL,
        name="extract",
    )(moving_block, partner, in_hbm(key_pool.reshape(pool)), in_hbm(value_pool.reshape(pool)))


def forward_kernel(partner, got, after, out):
    for replica in range(PIECES):
        out[replica] = got[partner[replica]]


def forward(partner, got, after):
    return pl.pallas_call(
        forward_kernel,
        out_shape=pltpu.VMEM(got.shape, got.dtype),
        in_specs=[SMEM, VMEM, VMEM],
        out_specs=VMEM,
        compiler_params=SMALL,
        name="forward",
    )(pltpu.with_memory_space_constraint(partner, pltpu.SMEM), in_vmem(got), after)


def picks(order):
    request = lax.broadcasted_iota(jnp.int32, (TOKG, TOKG), 0)
    return jnp.where(request == order, 1.0, 0.0).astype(jnp.bfloat16)


def rows_kernel(order, features, out, chosen, frame, near, rows, sems):
    odd = lax.axis_index("tp") % 2
    fetch = [
        pltpu.make_async_copy(order, near, sems.at[0]),
        pltpu.make_async_copy(
            features.at[0], frame.at[pl.ds(pl.multiple_of(odd * 64, 64), FEATS), :], sems.at[1]
        ),
    ]
    for copy in fetch:
        copy.start()
    blank = jnp.zeros((FRAME - FEATS, TOKG), jnp.bfloat16)
    frame[pl.ds(pl.multiple_of((1 - odd) * FEATS, 64), FRAME - FEATS), :] = blank
    fetch[0].wait()
    chosen[...] = picks(near[...])
    fetch[1].wait()
    picked = lax.dot_general(
        chosen[...], frame[...], (((0,), (1,)), ((), ())), preferred_element_type=jnp.float32
    )
    rows[...] = picked.astype(jnp.bfloat16).reshape(rows.shape)
    send = pltpu.make_async_copy(rows, out, sems.at[2])
    send.start()
    send.wait()


def slot_rows(order, projected):
    return pl.pallas_call(
        rows_kernel,
        out_shape=(
            jax.ShapeDtypeStruct((N_TP, ROWS, FRAME), jnp.bfloat16),
            pltpu.VMEM((TOKG, TOKG), jnp.bfloat16),
        ),
        in_specs=[HBM, HBM],
        out_specs=(HBM, VMEM),
        scratch_shapes=[
            pltpu.VMEM((FRAME, TOKG), jnp.bfloat16),
            pltpu.VMEM((1, TOKG), jnp.int32),
            pltpu.VMEM((N_TP, ROWS, FRAME), jnp.bfloat16),
            pltpu.SemaphoreType.DMA((3,)),
        ],
        cost_estimate=pl.CostEstimate(flops=2 * TOKG * TOKG * FRAME, bytes_accessed=400000, transcendentals=0),
        compiler_params=SMALL,
        name="slot_rows",
    )(in_hbm(order), in_hbm(projected))


def lanes(served, tile):
    pair, place = divmod(tile, 5)
    even, odd = 2 * pair, 2 * pair + 1
    if place < 2:
        return served[even, :, place * HD : (place + 1) * HD]
    if place > 2:
        return served[odd, :, (place - 2) * HD : (place - 1) * HD]
    return served[even, :, 2 * HD : 3 * HD] + served[odd, :, 0:HD]


def counts(tables, lengths, block, offset):
    total = jnp.zeros((ROWS, block.shape[1]), jnp.float32)
    for entry in range(TBL):
        hit = (tables[:, entry : entry + 1] == block) & (offset < lengths - entry * BLOCK)
        total = total + jnp.where(hit, 1.0, 0.0)
    return total


def attend_kernel(
    block_id, served, keys, value_pool, tables, lengths, numer, tops, totals, queries, moved, values, sem
):
    fetch = pltpu.make_async_copy(value_pool, values, sem)
    fetch.start()
    moved[...] = counts(
        jnp.where(tables[0] == block_id[...], 0, -1), lengths[...], jnp.zeros((1, BLOCK), jnp.int32),
        lax.broadcasted_iota(jnp.int32, (1, BLOCK), 1),
    )
    token = lax.broadcasted_iota(jnp.int32, (1, TOKENS), 1)
    block, offset = token // BLOCK, token % BLOCK
    block = jnp.where(block == block_id[...], -1, block)
    count = counts(tables[0], lengths[...], block, offset)
    kept = count > 0.0
    ones = jnp.ones((TOKENS, HD), jnp.bfloat16)
    for head in range(KVH):
        rows = jnp.concatenate([lanes(served, head * GROUP + g) for g in range(GROUP)], axis=0)
        queries[head] = rows
        fresh_key = lanes(served, H + head).astype(jnp.float32)
        fresh_value = lanes(served, H + KVH + head).astype(jnp.float32)
        cols = slice(head * HD, (head + 1) * HD)
        key = keys[0, :, :, cols].reshape(TOKENS, HD)
        score = lax.dot_general(rows, key, (((1,), (1,)), ((), ())), preferred_element_type=jnp.float32)
        score = jnp.where(kept[None], score.reshape(GROUP, ROWS, TOKENS), NEG)
        fresh = jnp.sum(
            rows.astype(jnp.float32).reshape(GROUP, ROWS, HD) * fresh_key[None], axis=-1, keepdims=True
        )
        top = jnp.maximum(jnp.max(score, axis=-1, keepdims=True), fresh)
        weight = jnp.exp2((score - top) * TO_EXP2).astype(jnp.bfloat16)
        weight = (weight.astype(jnp.float32) * count[None]).astype(jnp.bfloat16).reshape(GROUP * ROWS, TOKENS)
        if head == 0:
            fetch.wait()
        value = values[0, :, :, cols].reshape(TOKENS, HD)
        both = jnp.dot(weight, jnp.concatenate([value, ones], axis=1), preferred_element_type=jnp.float32)
        own = jnp.exp2((fresh - top) * TO_EXP2).astype(jnp.bfloat16).astype(jnp.float32)
        numer[head] = (both[:, :HD].reshape(GROUP, ROWS, HD) + own * fresh_value[None]).reshape(GROUP * ROWS, HD)
        total = both[:, HD:].reshape(GROUP, ROWS, HD) + own
        tops[head] = jnp.broadcast_to(top, (GROUP, ROWS, HD)).reshape(GROUP * ROWS, HD)
        totals[head] = total.reshape(GROUP * ROWS, HD)


def attend(moving_block, served, key_pool, value_pool, tables, lengths):
    rows = GROUP * ROWS
    return pl.pallas_call(
        attend_kernel,
        out_shape=(
            pltpu.VMEM((KVH, rows, HD), jnp.float32),
            pltpu.VMEM((KVH, rows, HD), jnp.float32),
            pltpu.VMEM((KVH, rows, HD), jnp.float32),
            pltpu.VMEM((KVH, rows, HD), jnp.bfloat16),
            pltpu.VMEM((ROWS, BLOCK), jnp.float32),
        ),
        in_specs=[VMEM, VMEM, VMEM, HBM, VMEM, VMEM],
        out_specs=(VMEM,) * 5,
        scratch_shapes=[
            pltpu.VMEM((1, NBLK, BLOCK, KVH * HD), jnp.bfloat16),
            pltpu.SemaphoreType.DMA,
        ],
        compiler_params=LARGE,
        cost_estimate=pl.CostEstimate(
            flops=4 * KVH * rows * TOKENS * HD, bytes_accessed=5000000, transcendentals=KVH * rows * TOKENS
        ),
        name="attend",
    )(moving_block, in_vmem(served), in_vmem(key_pool), in_hbm(value_pool), tables, lengths)


def merge_kernel(arrived, numer, tops, totals, queries, moved, out):
    count = moved[...]
    kept = count > 0.0
    ones = jnp.ones((BLOCK, HD), jnp.bfloat16)
    scores = []
    for head in range(KVH):
        key = jnp.concatenate([arrived[KVH * span + head] for span in range(SPANS)], axis=0)
        score = lax.dot_general(
            queries[head], key, (((1,), (1,)), ((), ())), preferred_element_type=jnp.float32
        )
        scores.append(jnp.where(kept[None], score.reshape(GROUP, ROWS, BLOCK), NEG))
    befores = [tops[head].reshape(GROUP, ROWS, HD) for head in range(KVH)]
    highest = [jnp.max(score, axis=-1, keepdims=True) for score in scores]
    latest = [jnp.maximum(new, old) for new, old in zip(highest, befores)]
    both = []
    for head in range(KVH):
        weight = jnp.exp2((scores[head] - latest[head][:, :, :BLOCK]) * TO_EXP2).astype(jnp.bfloat16)
        weight = (weight.astype(jnp.float32) * count[None]).astype(jnp.bfloat16).reshape(GROUP * ROWS, BLOCK)
        value = jnp.concatenate([arrived[KVH * (SPANS + span) + head] for span in range(SPANS)], axis=0)
        part = jnp.dot(weight, jnp.concatenate([value, ones], axis=1), preferred_element_type=jnp.float32)
        both.append(part.reshape(GROUP, ROWS, 2 * HD))
    results = []
    for head in range(KVH):
        kept_part = jnp.exp2((befores[head] - latest[head]) * TO_EXP2)
        top = numer[head].reshape(GROUP, ROWS, HD) * kept_part + both[head][:, :, :HD]
        bottom = totals[head].reshape(GROUP, ROWS, HD) * kept_part + both[head][:, :, HD:]
        results.append((top / bottom).astype(jnp.bfloat16))
    for head in range(KVH):
        for g in range(GROUP):
            out[4 * head + g // 2, :, (g % 2) * HD : (g % 2 + 1) * HD] = results[head][g]


def merge(arrived, numer, tops, totals, queries, moved):
    return pl.pallas_call(
        merge_kernel,
        out_shape=pltpu.VMEM((N_TP, ROWS, 2 * HD), jnp.bfloat16),
        in_specs=[VMEM] * 6,
        out_specs=VMEM,
        compiler_params=SMALL,
        name="merge",
    )(in_vmem(arrived), numer, tops, totals, queries, moved)


def place_kernel(chosen, returned, out, rows, sems):
    slots = returned[...].reshape(TOKG, 2 * HD)
    half = TOKG // 2
    copies = []
    for part in range(2):
        here = slice(part * half, (part + 1) * half)
        rows[here] = jnp.dot(chosen[here], slots, preferred_element_type=jnp.float32).astype(jnp.bfloat16)
        copies.append(pltpu.make_async_copy(rows.at[here], out.at[0, here], sems.at[part]))
        copies[-1].start()
    for copy in copies:
        copy.wait()


def place(chosen, returned):
    return pl.pallas_call(
        place_kernel,
        out_shape=jax.ShapeDtypeStruct((1, TOKG, 2 * HD), jnp.bfloat16),
        in_specs=[VMEM, VMEM],
        out_specs=HBM,
        scratch_shapes=[pltpu.VMEM((TOKG, 2 * HD), jnp.bfloat16), pltpu.SemaphoreType.DMA((2,))],
        compiler_params=SMALL,
        name="place",
    )(chosen, in_vmem(returned))


def exchange(slots, axis):
    return lax.all_to_all(slots, axis, split_axis=0, concat_axis=0, tiled=True)


def body(
    projected, serve_order, key_pool, value_pool, block_table, context_len, partner, moving_block
):
    lengths = context_len.reshape(ROWS, 1)
    rows, chosen = slot_rows(serve_order, jnp.swapaxes(projected, 1, 2))
    served = exchange(rows, "tp")
    pieces, mates = extract(key_pool, value_pool, moving_block, partner)
    spread = exchange(pieces, "rep")
    *parts, moved = attend(moving_block, served, key_pool, value_pool, block_table, lengths)
    arrived = exchange(forward(mates, spread, moved), "rep")
    return place(chosen, exchange(merge(arrived, *parts, moved), "tp"))


def solution(mesh):
    in_specs = (
        P("rep", None, "tp"),
        P("rep", None),
        P("rep", "tp", None, None),
        P("rep", "tp", None, None),
        P("rep", "tp", None),
        P("rep", "tp"),
        P(),
        P("rep", "tp"),
    )
    out_specs = P("rep", None, "tp")
    return jax.shard_map(body, mesh=mesh, in_specs=in_specs, out_specs=out_specs, check_vma=False)
```

```python
import math

import jax
import jax.numpy as jnp
from jax import lax
from jax.experimental import pallas as pl
from jax.experimental.pallas import tpu as pltpu
from jax.sharding import PartitionSpec as P

H = 32
KVH = 4
GROUP = H // KVH
HD = 128
BLOCK = 64
NBLK = 32
TBL = 8
ROWS = 16
TOKG = 256
N_TP = 16
FEATS = 320
FRAME = 384
PIECES = 32
SPANS = BLOCK // 16
TOKENS = NBLK * BLOCK
NEG = -1e30
TO_EXP2 = math.log2(math.e) / math.sqrt(HD)
VMEM = pl.BlockSpec(memory_space=pltpu.VMEM)
HBM = pl.BlockSpec(memory_space=pltpu.HBM)
SMEM = pl.BlockSpec(memory_space=pltpu.SMEM)
SMALL = pltpu.CompilerParams(vmem_limit_bytes=8 * 1024 * 1024)
LARGE = pltpu.CompilerParams(vmem_limit_bytes=24 * 1024 * 1024)


def in_vmem(array):
    return pltpu.with_memory_space_constraint(array, pltpu.VMEM)


def in_hbm(array):
    return pltpu.with_memory_space_constraint(array, pltpu.HBM)


def extract_kernel(block_id, partner, keys, values, out, mates, near, sems):
    for replica in range(PIECES):
        mates[replica] = partner[replica]
    copies = []
    for index in range(2 * SPANS):
        pool, span = (keys, values)[index // SPANS], index % SPANS
        copies.append(pltpu.make_async_copy(pool.at[block_id[0, 0], span], near.at[index], sems.at[index]))
        copies[-1].start()
    for index, copy in enumerate(copies):
        copy.wait()
        for head in range(KVH):
            out[KVH * index + head] = near[index, :, head * HD : (head + 1) * HD]


def extract(key_pool, value_pool, moving_block, partner):
    pool = (NBLK, SPANS, 16, KVH * HD)
    return pl.pallas_call(
        extract_kernel,
        out_shape=(pltpu.VMEM((PIECES, 16, HD), jnp.bfloat16), pltpu.SMEM((PIECES,), jnp.int32)),
        in_specs=[SMEM, SMEM, HBM, HBM],
        out_specs=(VMEM, SMEM),
        scratch_shapes=[
            pltpu.VMEM((2 * SPANS, 16, KVH * HD), jnp.bfloat16),
            pltpu.SemaphoreType.DMA((2 * SPANS,)),
        ],
        compiler_params=SMALL,
        name="extract",
    )(moving_block, partner, in_hbm(key_pool.reshape(pool)), in_hbm(value_pool.reshape(pool)))


def forward_kernel(partner, got, after, out):
    for replica in range(PIECES):
        out[replica] = got[partner[replica]]


def forward(partner, got, after):
    return pl.pallas_call(
        forward_kernel,
        out_shape=pltpu.VMEM(got.shape, got.dtype),
        in_specs=[SMEM, VMEM, VMEM],
        out_specs=VMEM,
        compiler_params=SMALL,
        name="forward",
    )(pltpu.with_memory_space_constraint(partner, pltpu.SMEM), in_vmem(got), after)


def rows_kernel(order, features, out, chosen, frame, near, rows, by_slot, sems):
    odd = lax.axis_index("tp") % 2
    fetch = [
        pltpu.make_async_copy(order, near, sems.at[0]),
        pltpu.make_async_copy(
            features.at[0], frame.at[pl.ds(pl.multiple_of(odd * 64, 64), FEATS), :], sems.at[1]
        ),
    ]
    for copy in fetch:
        copy.start()
    blank = jnp.zeros((FRAME - FEATS, TOKG), jnp.bfloat16)
    frame[pl.ds(pl.multiple_of((1 - odd) * FEATS, 64), FRAME - FEATS), :] = blank
    fetch[0].wait()
    request = lax.broadcasted_iota(jnp.int32, (TOKG, TOKG), 0)
    hits = jnp.where(request == near[...], 1.0, 0.0)
    chosen[...] = hits.astype(jnp.bfloat16)
    by_slot[...] = hits.T.astype(jnp.bfloat16)
    fetch[1].wait()
    send = []
    for part in range(2):
        width, slots = TOKG // 2, N_TP // 2
        picked = lax.dot_general(
            by_slot[part * width : (part + 1) * width],
            frame[...],
            (((1,), (1,)), ((), ())),
            preferred_element_type=jnp.float32,
        )
        here = pl.ds(part * slots, slots)
        rows[here] = picked.astype(jnp.bfloat16).reshape(slots, ROWS, FRAME)
        send.append(pltpu.make_async_copy(rows.at[here], out.at[here], sems.at[2 + part]))
        send[-1].start()
    for copy in send:
        copy.wait()


def slot_rows(order, projected):
    return pl.pallas_call(
        rows_kernel,
        out_shape=(
            jax.ShapeDtypeStruct((N_TP, ROWS, FRAME), jnp.bfloat16),
            pltpu.VMEM((TOKG, TOKG), jnp.bfloat16),
        ),
        in_specs=[HBM, HBM],
        out_specs=(HBM, VMEM),
        scratch_shapes=[
            pltpu.VMEM((FRAME, TOKG), jnp.bfloat16),
            pltpu.VMEM((1, TOKG), jnp.int32),
            pltpu.VMEM((N_TP, ROWS, FRAME), jnp.bfloat16),
            pltpu.VMEM((TOKG, TOKG), jnp.bfloat16),
            pltpu.SemaphoreType.DMA((4,)),
        ],
        cost_estimate=pl.CostEstimate(flops=2 * TOKG * TOKG * FRAME, bytes_accessed=400000, transcendentals=0),
        compiler_params=SMALL,
        name="slot_rows",
    )(in_hbm(order), in_hbm(projected))


def lanes(served, tile):
    pair, place = divmod(tile, 5)
    even, odd = 2 * pair, 2 * pair + 1
    if place < 2:
        return served[even, :, place * HD : (place + 1) * HD]
    if place > 2:
        return served[odd, :, (place - 2) * HD : (place - 1) * HD]
    return served[even, :, 2 * HD : 3 * HD] + served[odd, :, 0:HD]


def counts(tables, lengths, block, offset):
    total = jnp.zeros((ROWS, block.shape[1]), jnp.float32)
    for entry in range(TBL):
        hit = (tables[:, entry : entry + 1] == block) & (offset < lengths - entry * BLOCK)
        total = total + jnp.where(hit, 1.0, 0.0)
    return total


def attend_kernel(
    block_id, served, keys, value_pool, tables, lengths, numer, tops, totals, queries, moved, values, sem
):
    fetch = pltpu.make_async_copy(value_pool, values, sem)
    fetch.start()
    moved[...] = counts(
        jnp.where(tables[0] == block_id[...], 0, -1), lengths[...], jnp.zeros((1, BLOCK), jnp.int32),
        lax.broadcasted_iota(jnp.int32, (1, BLOCK), 1),
    )
    token = lax.broadcasted_iota(jnp.int32, (1, TOKENS), 1)
    block, offset = token // BLOCK, token % BLOCK
    block = jnp.where(block == block_id[...], -1, block)
    count = counts(tables[0], lengths[...], block, offset)
    kept = count > 0.0
    ones = jnp.ones((TOKENS, HD), jnp.bfloat16)
    for head in range(KVH):
        rows = jnp.concatenate([lanes(served, head * GROUP + g) for g in range(GROUP)], axis=0)
        queries[head] = rows
        fresh_key = lanes(served, H + head).astype(jnp.float32)
        fresh_value = lanes(served, H + KVH + head).astype(jnp.float32)
        cols = slice(head * HD, (head + 1) * HD)
        key = keys[0, :, :, cols].reshape(TOKENS, HD)
        score = lax.dot_general(rows, key, (((1,), (1,)), ((), ())), preferred_element_type=jnp.float32)
        score = jnp.where(kept[None], score.reshape(GROUP, ROWS, TOKENS), NEG)
        fresh = jnp.sum(
            rows.astype(jnp.float32).reshape(GROUP, ROWS, HD) * fresh_key[None], axis=-1, keepdims=True
        )
        top = jnp.maximum(jnp.max(score, axis=-1, keepdims=True), fresh)
        weight = jnp.exp2((score - top) * TO_EXP2).astype(jnp.bfloat16)
        weight = (weight.astype(jnp.float32) * count[None]).astype(jnp.bfloat16).reshape(GROUP * ROWS, TOKENS)
        if head == 0:
            fetch.wait()
        value = values[0, :, :, cols].reshape(TOKENS, HD)
        both = jnp.dot(weight, jnp.concatenate([value, ones], axis=1), preferred_element_type=jnp.float32)
        own = jnp.exp2((fresh - top) * TO_EXP2).astype(jnp.bfloat16).astype(jnp.float32)
        numer[head] = (both[:, :HD].reshape(GROUP, ROWS, HD) + own * fresh_value[None]).reshape(GROUP * ROWS, HD)
        total = both[:, HD:].reshape(GROUP, ROWS, HD) + own
        tops[head] = jnp.broadcast_to(top, (GROUP, ROWS, HD)).reshape(GROUP * ROWS, HD)
        totals[head] = total.reshape(GROUP * ROWS, HD)


def attend(moving_block, served, key_pool, value_pool, tables, lengths):
    rows = GROUP * ROWS
    return pl.pallas_call(
        attend_kernel,
        out_shape=(
            pltpu.VMEM((KVH, rows, HD), jnp.float32),
            pltpu.VMEM((KVH, rows, HD), jnp.float32),
            pltpu.VMEM((KVH, rows, HD), jnp.float32),
            pltpu.VMEM((KVH, rows, HD), jnp.bfloat16),
            pltpu.VMEM((ROWS, BLOCK), jnp.float32),
        ),
        in_specs=[VMEM, VMEM, VMEM, HBM, VMEM, VMEM],
        out_specs=(VMEM,) * 5,
        scratch_shapes=[
            pltpu.VMEM((1, NBLK, BLOCK, KVH * HD), jnp.bfloat16),
            pltpu.SemaphoreType.DMA,
        ],
        compiler_params=LARGE,
        cost_estimate=pl.CostEstimate(
            flops=4 * KVH * rows * TOKENS * HD, bytes_accessed=5000000, transcendentals=KVH * rows * TOKENS
        ),
        name="attend",
    )(moving_block, in_vmem(served), in_vmem(key_pool), in_hbm(value_pool), tables, lengths)


def merge_kernel(arrived, numer, tops, totals, queries, moved, out):
    count = moved[...]
    kept = count > 0.0
    ones = jnp.ones((BLOCK, HD), jnp.bfloat16)
    scores = []
    for head in range(KVH):
        key = jnp.concatenate([arrived[KVH * span + head] for span in range(SPANS)], axis=0)
        score = lax.dot_general(
            queries[head], key, (((1,), (1,)), ((), ())), preferred_element_type=jnp.float32
        )
        scores.append(jnp.where(kept[None], score.reshape(GROUP, ROWS, BLOCK), NEG))
    befores = [tops[head].reshape(GROUP, ROWS, HD) for head in range(KVH)]
    highest = [jnp.max(score, axis=-1, keepdims=True) for score in scores]
    latest = [jnp.maximum(new, old) for new, old in zip(highest, befores)]
    both = []
    for head in range(KVH):
        weight = jnp.exp2((scores[head] - latest[head][:, :, :BLOCK]) * TO_EXP2).astype(jnp.bfloat16)
        weight = (weight.astype(jnp.float32) * count[None]).astype(jnp.bfloat16).reshape(GROUP * ROWS, BLOCK)
        value = jnp.concatenate([arrived[KVH * (SPANS + span) + head] for span in range(SPANS)], axis=0)
        part = jnp.dot(weight, jnp.concatenate([value, ones], axis=1), preferred_element_type=jnp.float32)
        both.append(part.reshape(GROUP, ROWS, 2 * HD))
    results = []
    for head in range(KVH):
        kept_part = jnp.exp2((befores[head] - latest[head]) * TO_EXP2)
        top = numer[head].reshape(GROUP, ROWS, HD) * kept_part + both[head][:, :, :HD]
        bottom = totals[head].reshape(GROUP, ROWS, HD) * kept_part + both[head][:, :, HD:]
        results.append((top / bottom).astype(jnp.bfloat16))
    for head in range(KVH):
        for g in range(GROUP):
            out[4 * head + g // 2, :, (g % 2) * HD : (g % 2 + 1) * HD] = results[head][g]


def merge(arrived, numer, tops, totals, queries, moved):
    return pl.pallas_call(
        merge_kernel,
        out_shape=pltpu.VMEM((N_TP, ROWS, 2 * HD), jnp.bfloat16),
        in_specs=[VMEM] * 6,
        out_specs=VMEM,
        compiler_params=SMALL,
        name="merge",
    )(in_vmem(arrived), numer, tops, totals, queries, moved)


def place_kernel(chosen, returned, out, rows, sems):
    slots = returned[...].reshape(TOKG, 2 * HD)
    half = TOKG // 2
    copies = []
    for part in range(2):
        here = slice(part * half, (part + 1) * half)
        rows[here] = jnp.dot(chosen[here], slots, preferred_element_type=jnp.float32).astype(jnp.bfloat16)
        copies.append(pltpu.make_async_copy(rows.at[here], out.at[0, here], sems.at[part]))
        copies[-1].start()
    for copy in copies:
        copy.wait()


def place(chosen, returned):
    return pl.pallas_call(
        place_kernel,
        out_shape=jax.ShapeDtypeStruct((1, TOKG, 2 * HD), jnp.bfloat16),
        in_specs=[VMEM, VMEM],
        out_specs=HBM,
        scratch_shapes=[pltpu.VMEM((TOKG, 2 * HD), jnp.bfloat16), pltpu.SemaphoreType.DMA((2,))],
        compiler_params=SMALL,
        name="place",
    )(chosen, in_vmem(returned))


def exchange(slots, axis):
    return lax.all_to_all(slots, axis, split_axis=0, concat_axis=0, tiled=True)


def body(
    projected, serve_order, key_pool, value_pool, block_table, context_len, partner, moving_block
):
    lengths = context_len.reshape(ROWS, 1)
    rows, chosen = slot_rows(serve_order, jnp.swapaxes(projected, 1, 2))
    served = exchange(rows, "tp")
    pieces, mates = extract(key_pool, value_pool, moving_block, partner)
    spread = exchange(pieces, "rep")
    *parts, moved = attend(moving_block, served, key_pool, value_pool, block_table, lengths)
    arrived = exchange(forward(mates, spread, moved), "rep")
    return place(chosen, exchange(merge(arrived, *parts, moved), "tp"))


def solution(mesh):
    in_specs = (
        P("rep", None, "tp"),
        P("rep", None),
        P("rep", "tp", None, None),
        P("rep", "tp", None, None),
        P("rep", "tp", None),
        P("rep", "tp"),
        P(),
        P("rep", "tp"),
    )
    out_specs = P("rep", None, "tp")
    return jax.shard_map(body, mesh=mesh, in_specs=in_specs, out_specs=out_specs, check_vma=False)
```
